32 devices in a mesh: groups: 2 (over y), wide: 16 (over z, x, core).
Axes of the slice: x: 2, y: 2, z: 4, core: 2. Of those that a mesh axis runs over, the one named last changes fastest.
Arguments:
- fields: bfloat16 [32, 512], P(('groups', 'wide')), parts along dimension 0, may hold values from -6 to 6
- chol: bfloat16 [512, 1024, 1024], P(None, 'wide'), may hold values from -0.01171875 to 0.01171875
- orbitals: bfloat16 [32, 1024, 256], P(('groups', 'wide')), parts along dimension 0, may hold values from -6 to 6
- trial: bfloat16 [1024, 256], replicated, may hold values from -0.5 to 0.5
Outputs:
- new_orbitals: bfloat16 [32, 1024, 256], P(('groups', 'wide')), parts along dimension 0
- force_bias: float32 [32, 2, 512], P(('groups', 'wide')), parts along dimension 0
The draws below stay inside these ranges and needn't reach their ends.
There are 2 independent parts, one for each index of `groups`. The reference program is written for one: setup_inputs(seed, part) draws one part's arguments, and reference() takes and returns one part's arrays. A program takes and returns all parts, laid end to end along the dimension named above; an argument that names none is the same for every part. Nothing has to cross between parts.
All inputs are finite; a program needn't handle non-finite values.
Results may differ from the reference program's by a relative error of at most 0.0075.
Values may be sent and summed in bfloat16 or wider, within the bound.
A program may use at most 192 MiB of HBM per device.

```python
import jax
import jax.numpy as jnp
from jax import lax

N = 1024
NOCC = 128
NG = 512
TAYLOR = 4
WALKERS = 16


def level_of(key, extent, pieces, least, top_value):
    factor_of = 1.0
    for dim, parts in pieces:
        steps = jax.random.uniform(jax.random.fold_in(jax.random.fold_in(key, 6), dim), (parts,), jnp.float32, least / len(pieces), top_value / len(pieces))
        factor_of = factor_of * jnp.repeat(jnp.exp(steps), extent[dim] // parts).reshape((-1,) + (1,) * (len(extent) - 1 - dim))
    return factor_of


def bell_draw(rng, dims, scale, bound, split=(), kind=jnp.bfloat16):
    loudness = level_of(rng, dims, split, -0.22, 0.18) if split else 1.0
    entries = jax.random.normal(rng, dims, jnp.float32) * scale * loudness
    return jnp.minimum(jnp.maximum(entries, -bound), bound).astype(kind)


def setup_inputs(seed: int = 0, part: int = 0) -> dict:
    streams_of = jax.random.split(jax.random.key(seed), 5)
    part_keys = jax.random.split(jax.random.fold_in(streams_of[4], part), 5)
    fields = bell_draw(part_keys[0], (WALKERS, NG), 1.0, 6.0, ((0, 16),))
    chol = bell_draw(streams_of[1], (NG, N, N), (N * NG // 2) ** -0.5, 0.01171875, ((1, 16),))
    orbitals = bell_draw(part_keys[2], (WALKERS, N, 2 * NOCC), 1.0, 6.0, ((0, 16),))
    trial = bell_draw(streams_of[3], (N, 2 * NOCC), NOCC ** -0.5, 0.5)
    return {"fields": fields, "chol": chol, "orbitals": orbitals, "trial": trial}


def reference(fields, chol, orbitals, trial):
    chol_flat = chol.reshape(NG, N * N)
    generator = jnp.dot(fields, chol_flat, preferred_element_type=jnp.float32).astype(jnp.bfloat16).reshape(WALKERS, N, N)
    trial_real = trial[:, :NOCC].T
    trial_imag = trial[:, NOCC:].T
    mixer = jnp.concatenate([jnp.concatenate([trial_real, -trial_imag], axis=1), jnp.concatenate([trial_imag, trial_real], axis=1)], axis=0)

    def propagate(inputs):
        gen_walker, orb_walker = inputs
        total = orb_walker.astype(jnp.float32)
        operand = orb_walker
        for order in range(1, TAYLOR + 1):
            product = jnp.dot(gen_walker, operand, preferred_element_type=jnp.float32)
            term = jnp.concatenate([-product[:, NOCC:], product[:, :NOCC]], axis=1) / order
            total = total + term
            operand = term.astype(jnp.bfloat16)
        fresh = total.astype(jnp.bfloat16)
        green = jnp.dot(fresh, mixer, preferred_element_type=jnp.float32).astype(jnp.bfloat16)
        paired = jnp.stack([green[:, :N].reshape(-1), green[:, N:].reshape(-1)], axis=0)
        return fresh, paired

    new_orbitals, greens = lax.map(propagate, (generator, orbitals))
    greens = greens.reshape(WALKERS * 2, N * N)
    bias = jnp.dot(greens, chol_flat.T, preferred_element_type=jnp.float32)
    force_bias = bias.reshape(WALKERS, 2, NG)
    return new_orbitals, force_bias
```

```python
import functools

import jax
import jax.numpy as jnp
from jax import lax
from jax.experimental import pallas as pl
from jax.experimental.pallas import tpu as pltpu
from jax.sharding import PartitionSpec as P

TAYLOR = 4
SUB = 8
LANES = 128
MESH = pl.DeviceIdType.MESH
NT = (((1,), (1,)), ((), ()))


def kernel(
    n, halves, slots, row_block,
    fld, chol, orb, trial, out, bias,
    fall, kron, held, accum, gen_local, gen_all, total, operand, orb_rows, orb_wide,
    green, scores, fb, fb_all, load_sem, send_sem, recv_sem,
):
    me = lax.axis_index("wide")
    vectors, rows, width = chol.shape
    half_vectors = vectors // halves
    units = (rows // row_block) * halves
    subs = row_block // SUB
    walkers = n
    depth = half_vectors * SUB
    cols = 256
    groups_q = vectors // LANES

    def load(unit):
        b, gh = unit // halves, lax.rem(unit, halves)
        return pltpu.make_async_copy(
            chol.at[pl.ds(gh * half_vectors, half_vectors), pl.ds(b * row_block, row_block), :],
            held.at[lax.rem(unit, slots)],
            load_sem.at[lax.rem(unit, slots)],
        )

    def start_load(unit, _=None):
        load(unit).start()

    def peers(body):
        lax.fori_loop(1, n, lambda k, c: (body(lax.rem(me + k, n)), c)[1], 0)

    def send(src, dst, which, peer):
        pltpu.make_async_remote_copy(
            src_ref=src, dst_ref=dst, send_sem=send_sem.at[which], recv_sem=recv_sem.at[which],
            device_id={"wide": peer}, device_id_type=MESH,
        ).start()

    def wait_all(ref, sem):
        part = ref.at[pl.ds(0, n - 1)]
        pltpu.make_async_copy(part, part, sem).wait()

    lax.fori_loop(0, slots, lambda u, c: (start_load(u), c)[1], 0)

    barrier = pltpu.get_barrier_semaphore()
    peers(lambda p: pl.semaphore_signal(barrier, inc=1, device_id={"wide": p}, device_id_type=MESH))
    pl.semaphore_wait(barrier, n - 1)

    peers(lambda p: send(fld, fall.at[me], 0, p))
    fall[me] = fld[...]
    wait_all(fall, recv_sem.at[0])

    span = LANES * SUB
    spread = (
        lax.broadcasted_iota(jnp.int32, (LANES, span), 1) >> 3
        == lax.broadcasted_iota(jnp.int32, (LANES, span), 0)
    ).astype(jnp.bfloat16)
    diagonal = (lax.broadcasted_iota(jnp.int32, (walkers * SUB, span), 1) & (SUB - 1)) == (
        lax.broadcasted_iota(jnp.int32, (walkers * SUB, span), 0) & (SUB - 1)
    )
    for q in range(groups_q):
        line = jnp.broadcast_to(fall[:, q : q + 1, :], (walkers, SUB, LANES))
        line = line.reshape(walkers * SUB, LANES).astype(jnp.bfloat16)
        wide = jnp.dot(line, spread, preferred_element_type=jnp.float32)
        kron[:, q * span : (q + 1) * span] = jnp.where(diagonal, wide, 0.0).astype(jnp.bfloat16)

    def generate(unit, carry):
        b, gh = unit // halves, lax.rem(unit, halves)
        slot = lax.rem(unit, slots)
        load(unit).wait()

        @pl.when(gh == 0)
        def _():
            accum[...] = jnp.zeros_like(accum)

        for h in range(subs):

            def column(jc, c):
                at = pl.ds(pl.multiple_of(jc * cols, cols), cols)
                right = held[slot, :, h * SUB : (h + 1) * SUB, at].reshape(depth, cols)
                left = kron[:, pl.ds(pl.multiple_of(gh * depth, depth), depth)]
                got = jnp.dot(left, right, preferred_element_type=jnp.float32)
                accum[:, h * SUB : (h + 1) * SUB, at] += got.reshape(walkers, SUB, cols)
                return c

            lax.fori_loop(0, width // cols, column, 0)

        @pl.when(unit + slots < units)
        def _():
            start_load(unit + slots)

        @pl.when(gh == halves - 1)
        def _():
            at = pl.ds(pl.multiple_of(b * row_block, row_block), row_block)
            gen_local[:, at, :] = accum[...].astype(jnp.bfloat16)
            peers(lambda p: send(gen_local.at[p, at], gen_all.at[me, at], 1, p))
            gen_all[me, at, :] = gen_local[me, at, :]

        return carry

    lax.fori_loop(0, units, generate, 0)

    scores[...] = jnp.zeros_like(scores)
    fb[...] = jnp.zeros_like(fb)
    wait_all(gen_all, recv_sem.at[1])

    size = orb.shape[0]
    nocc = orb.shape[1] // 2
    tile = 256
    per_tile = tile // rows
    for order in range(1, TAYLOR + 1):

        def advance(i, c, order=order):
            at = pl.ds(pl.multiple_of(i * tile, tile), tile)
            gen = gen_all[pl.ds(i * per_tile, per_tile), :, :].reshape(tile, size)
            before = orb[...] if order == 1 else operand[order % 2]
            product = jnp.dot(gen, before, preferred_element_type=jnp.float32)
            term = jnp.concatenate([-product[:, nocc:], product[:, :nocc]], axis=1) / order
            if order == 1:
                now = orb[at, :].astype(jnp.float32) + term
            else:
                now = total[at, :] + term
            if order < TAYLOR:
                total[at, :] = now
                operand[(order + 1) % 2, at, :] = term.astype(jnp.bfloat16)
            else:
                out[pl.ds(i * per_tile, per_tile), :, :] = now.reshape(
                    per_tile, rows, 2 * nocc
                ).astype(jnp.bfloat16)
            return c

        lax.fori_loop(0, size // tile, advance, 0)

    peers(lambda p: send(out.at[p], orb_rows.at[me], 2, p))
    orb_rows[me] = out[me]
    wait_all(orb_rows, recv_sem.at[2])

    orb_wide[...] = orb_rows[...].astype(jnp.float32)

    def make_green(r, c):
        at = pl.ds(pl.multiple_of(r * SUB, SUB), SUB)
        block = orb_wide[:, at, :].reshape(walkers * SUB, 2 * nocc)
        turned = jnp.concatenate([block[:, nocc:], -block[:, :nocc]], axis=1)
        both = jnp.concatenate([block, turned], axis=0).astype(jnp.bfloat16)
        green[r] = lax.dot_general(
            trial[...], both, NT, preferred_element_type=jnp.float32
        ).astype(jnp.bfloat16)
        return c

    lax.fori_loop(0, rows // SUB, make_green, 0)

    chunk = 64
    many = 2 * walkers * SUB
    take = min(many, 256)
    for nc in range(many // take):
        if nc:
            scores[...] = jnp.zeros_like(scores)

        def contract(step, carry, nc=nc):
            unit = lax.rem(units - slots + step, units)
            b, gh = unit // halves, lax.rem(unit, halves)
            slot = lax.rem(unit, slots)

            if slots < units:

                @pl.when(step >= slots)
                def _():
                    load(unit).wait()

            def piece(i, c):
                got = None
                for h in range(subs):
                    left = held[slot, pl.ds(i * chunk, chunk), h * SUB : (h + 1) * SUB, :]
                    add = jnp.dot(
                        left.reshape(chunk * SUB, width),
                        green[b * subs + h, :, nc * take : (nc + 1) * take],
                        preferred_element_type=jnp.float32,
                    )
                    got = add if got is None else got + add
                at = pl.ds(pl.multiple_of(gh * depth + i * chunk * SUB, SUB), chunk * SUB)
                scores[at, :] += got
                return c

            lax.fori_loop(0, half_vectors // chunk, piece, 0)

            if slots < units:

                @pl.when(step + slots < units)
                def _():
                    start_load(step)

            return carry

        lax.fori_loop(0, units, contract, 0)

        own = (lax.broadcasted_iota(jnp.int32, (SUB, take), 1) & (SUB - 1)) == (
            lax.broadcasted_iota(jnp.int32, (SUB, take), 0)
        )
        lines = fb.shape[1]
        walker = lax.broadcasted_iota(jnp.int32, (walkers, lines, take), 0)
        line = lax.broadcasted_iota(jnp.int32, (walkers, lines, take), 1)
        source = (lax.broadcasted_iota(jnp.int32, (walkers, lines, take), 2) + nc * take) >> 3
        for q in range(groups_q):
            part = scores[q * span : (q + 1) * span, :].reshape(LANES, SUB, take)
            part = jnp.sum(jnp.where(own[None], part, 0.0), axis=1)
            pick = ((line == q) & (source == walker)) | (
                (line == groups_q + q) & (source == walkers + walker)
            )
            pick = pick.astype(jnp.float32).reshape(walkers * lines, take)
            fb[...] += lax.dot_general(
                pick, part, NT, preferred_element_type=jnp.float32, precision=lax.Precision.HIGHEST
            ).reshape(walkers, lines, LANES)

    peers(lambda p: send(fb.at[p], fb_all.at[me], 3, p))
    fb_all[me] = fb[me]
    wait_all(fb_all, recv_sem.at[3])
    bias[...] = jnp.sum(fb_all[...], axis=0)

    wait_all(fall, send_sem.at[0])
    wait_all(gen_local, send_sem.at[1])
    wait_all(orb_rows, send_sem.at[2])
    wait_all(fb, send_sem.at[3])


def per_device(n, fields, chol, orbitals, trial):
    vectors, rows, width = chol.shape
    size, both = orbitals.shape[1:]
    row_block = min(16, rows)
    halves = 2
    units = (rows // row_block) * halves
    slots = min(4, units)
    q = vectors // LANES
    lines = -(-q // 8) * 8
    fb_lines = -(-2 * q // 8) * 8
    fld = jnp.pad(fields.astype(jnp.float32).reshape(q, LANES), ((0, lines - q), (0, 0)))
    vmem = pl.BlockSpec(memory_space=pltpu.VMEM)
    bf16, f32 = jnp.bfloat16, jnp.float32
    out, bias = pl.pallas_call(
        functools.partial(kernel, n, halves, slots, row_block),
        out_shape=(
            jax.ShapeDtypeStruct((n, rows, both), bf16),
            jax.ShapeDtypeStruct((fb_lines, LANES), f32),
        ),
        in_specs=[vmem, pl.BlockSpec(memory_space=pl.ANY), vmem, vmem],
        out_specs=(vmem, vmem),
        scratch_shapes=[
            pltpu.VMEM((n, lines, LANES), f32),
            pltpu.VMEM((n * SUB, vectors * SUB), bf16),
            pltpu.VMEM((slots, vectors // halves, row_block, width), bf16),
            pltpu.VMEM((n, row_block, width), f32),
            pltpu.VMEM((n, rows, width), bf16),
            pltpu.VMEM((n, rows, width), bf16),
            pltpu.VMEM((size, both), f32),
            pltpu.VMEM((2, size, both), bf16),
            pltpu.VMEM((n, rows, both), bf16),
            pltpu.VMEM((n, rows, both), f32),
            pltpu.VMEM((rows // SUB, width, 2 * n * SUB), bf16),
            pltpu.VMEM((vectors * SUB, min(2 * n * SUB, 256)), f32),
            pltpu.VMEM((n, fb_lines, LANES), f32),
            pltpu.VMEM((n, fb_lines, LANES), f32),
            pltpu.SemaphoreType.DMA((slots,)),
            pltpu.SemaphoreType.DMA((4,)),
            pltpu.SemaphoreType.DMA((4,)),
        ],
        compiler_params=pltpu.CompilerParams(
            collective_id=0, has_side_effects=True, vmem_limit_bytes=60 * 1024 * 1024
        ),
    )(fld, chol, orbitals[0], trial)
    return (
        out.reshape(1, size, both),
        bias[: 2 * q].reshape(1, 2, vectors),
    )


def solution(mesh):
    in_specs = (
        P(("groups", "wide"), None),
        P(None, "wide", None),
        P(("groups", "wide"), None, None),
        P(),
    )
    out_specs = (P(("groups", "wide"), None, None), P(("groups", "wide"), None, None))
    return jax.shard_map(
        functools.partial(per_device, mesh.shape["wide"]),
        mesh=mesh, in_specs=in_specs, out_specs=out_specs, check_vma=False,
    )
```

```python
import functools

import jax
import jax.numpy as jnp
from jax import lax
from jax.experimental import pallas as pl
from jax.experimental.pallas import tpu as pltpu
from jax.sharding import PartitionSpec as P

TAYLOR = 4
SUB = 8
LANES = 128
MESH = pl.DeviceIdType.MESH
NT = (((1,), (1,)), ((), ()))


def kernel(
    n, halves, slots, row_block,
    fields, chol, orb, trial, out, bias,
    fld, fall, kron, held, accum, gen_local, gen_all, total, operand, orb_rows, orb_wide,
    green, scores, fb, fb_all, load_sem, send_sem, recv_sem, orb_sem,
):
    me = lax.axis_index("wide")
    vectors, rows, width = chol.shape
    half_vectors = vectors // halves
    units = (rows // row_block) * halves
    subs = row_block // SUB
    walkers = n
    depth = half_vectors * SUB
    cols = 256
    groups_q = vectors // LANES

    def load(unit):
        b, gh = unit // halves, lax.rem(unit, halves)
        return pltpu.make_async_copy(
            chol.at[pl.ds(gh * half_vectors, half_vectors), pl.ds(b * row_block, row_block), :],
            held.at[lax.rem(unit, slots)],
            load_sem.at[lax.rem(unit, slots)],
        )

    def start_load(unit, _=None):
        load(unit).start()

    def peers(body):
        lax.fori_loop(1, n, lambda k, c: (body(lax.rem(me + k, n)), c)[1], 0)

    def far_first(body):
        half = n // 2
        side = me // half
        across, here = (1 - side) * half, side * half
        lax.fori_loop(0, half, lambda k, c: (body(across + lax.rem(me + k, half)), c)[1], 0)
        lax.fori_loop(1, half, lambda k, c: (body(here + lax.rem(me + k, half)), c)[1], 0)

    def send(src, dst, which, peer, arrived=None):
        pltpu.make_async_remote_copy(
            src_ref=src, dst_ref=dst, send_sem=send_sem.at[which],
            recv_sem=recv_sem.at[which] if arrived is None else arrived,
            device_id={"wide": peer}, device_id_type=MESH,
        ).start()

    def wait_all(ref, sem):
        part = ref.at[pl.ds(0, n - 1)]
        pltpu.make_async_copy(part, part, sem).wait()

    lax.fori_loop(0, slots, lambda u, c: (start_load(u), c)[1], 0)

    barrier = pltpu.get_barrier_semaphore()
    peers(lambda p: pl.semaphore_signal(barrier, inc=1, device_id={"wide": p}, device_id_type=MESH))
    pl.semaphore_wait(barrier, n - 1)

    fld[...] = jnp.zeros_like(fld)
    for q in range(groups_q):
        fld[q : q + 1, :] = fields[:, q * LANES : (q + 1) * LANES].astype(jnp.float32)
    peers(lambda p: send(fld, fall.at[me], 0, p))
    fall[me] = fld[...]
    wait_all(fall, recv_sem.at[0])

    span = LANES * SUB
    spread = (
        lax.broadcasted_iota(jnp.int32, (LANES, span), 1) >> 3
        == lax.broadcasted_iota(jnp.int32, (LANES, span), 0)
    ).astype(jnp.bfloat16)
    diagonal = (lax.broadcasted_iota(jnp.int32, (walkers * SUB, span), 1) & (SUB - 1)) == (
        lax.broadcasted_iota(jnp.int32, (walkers * SUB, span), 0) & (SUB - 1)
    )
    for q in range(groups_q):
        line = jnp.broadcast_to(fall[:, q : q + 1, :], (walkers, SUB, LANES))
        line = line.reshape(walkers * SUB, LANES).astype(jnp.bfloat16)
        wide = jnp.dot(line, spread, preferred_element_type=jnp.float32)
        kron[:, q * span : (q + 1) * span] = jnp.where(diagonal, wide, 0.0).astype(jnp.bfloat16)

    def generate(unit, carry):
        b, gh = unit // halves, lax.rem(unit, halves)
        slot = lax.rem(unit, slots)
        load(unit).wait()

        @pl.when(gh == 0)
        def _():
            accum[...] = jnp.zeros_like(accum)

        for h in range(subs):

            def column(jc, c):
                at = pl.ds(pl.multiple_of(jc * cols, cols), cols)
                right = held[slot, :, h * SUB : (h + 1) * SUB, at].reshape(depth, cols)
                left = kron[:, pl.ds(pl.multiple_of(gh * depth, depth), depth)]
                got = jnp.dot(left, right, preferred_element_type=jnp.float32)
                accum[:, h * SUB : (h + 1) * SUB, at] += got.reshape(walkers, SUB, cols)
                return c

            lax.fori_loop(0, width // cols, column, 0)

        @pl.when(unit + slots < units)
        def _():
            start_load(unit + slots)

        @pl.when(gh == halves - 1)
        def _():
            at = pl.ds(pl.multiple_of(b * row_block, row_block), row_block)
            gen_local[:, at, :] = accum[...].astype(jnp.bfloat16)
            far_first(lambda p: send(gen_local.at[p, at], gen_all.at[me, at], 1, p))
            gen_all[me, at, :] = gen_local[me, at, :]

        return carry

    lax.fori_loop(0, units, generate, 0)

    scores[...] = jnp.zeros_like(scores)
    fb[...] = jnp.zeros_like(fb)
    wait_all(gen_all, recv_sem.at[1])

    size = orb.shape[0]
    nocc = orb.shape[1] // 2
    tile = 256
    per_tile = tile // rows
    for order in range(1, TAYLOR + 1):

        def advance(i, c, order=order):
            at = pl.ds(pl.multiple_of(i * tile, tile), tile)
            gen = gen_all[pl.ds(i * per_tile, per_tile), :, :].reshape(tile, size)
            before = orb[...] if order == 1 else operand[order % 2]
            product = jnp.dot(gen, before, preferred_element_type=jnp.float32)
            term = jnp.concatenate([-product[:, nocc:], product[:, :nocc]], axis=1) / order
            if order == 1:
                now = orb[at, :].astype(jnp.float32) + term
            else:
                now = total[at, :] + term
            if order < TAYLOR:
                total[at, :] = now
                operand[(order + 1) % 2, at, :] = term.astype(jnp.bfloat16)
            else:
                out[pl.ds(i * per_tile, per_tile), :, :] = now.reshape(
                    per_tile, rows, 2 * nocc
                ).astype(jnp.bfloat16)
            return c

        lax.fori_loop(0, size // tile, advance, 0)

    blocks = rows // row_block
    first = (units - slots) // halves
    for step in range(blocks):
        b = (first + step) % blocks
        at = pl.ds(b * row_block, row_block)
        far_first(lambda p, at=at, b=b: send(out.at[p, at], orb_rows.at[me, at], 2, p, orb_sem.at[b]))
    orb_rows[me] = out[me]

    def make_green(b):
        at = pl.ds(pl.multiple_of(b * row_block, row_block), row_block)
        part = orb_rows.at[pl.ds(0, n - 1), at]
        pltpu.make_async_copy(part, part, orb_sem.at[b]).wait()
        orb_wide[...] = orb_rows[:, at, :].astype(jnp.float32)
        for h in range(subs):
            block = orb_wide[:, h * SUB : (h + 1) * SUB, :].reshape(walkers * SUB, 2 * nocc)
            turned = jnp.concatenate([block[:, nocc:], -block[:, :nocc]], axis=1)
            both = jnp.concatenate([block, turned], axis=0).astype(jnp.bfloat16)
            green[b * subs + h] = lax.dot_general(
                trial[...], both, NT, preferred_element_type=jnp.float32
            ).astype(jnp.bfloat16)

    chunk = 64
    many = 2 * walkers * SUB
    take = min(many, 256)
    for nc in range(many // take):
        if nc:
            scores[...] = jnp.zeros_like(scores)

        def contract(step, carry, nc=nc):
            unit = lax.rem(units - slots + step, units)
            b, gh = unit // halves, lax.rem(unit, halves)
            slot = lax.rem(unit, slots)

            if nc == 0:

                @pl.when(gh == 0)
                def _():
                    make_green(b)

            if slots < units:

                @pl.when(step >= slots)
                def _():
                    load(unit).wait()

            def piece(i, c):
                got = None
                for h in range(subs):
                    left = held[slot, pl.ds(i * chunk, chunk), h * SUB : (h + 1) * SUB, :]
                    add = jnp.dot(
                        left.reshape(chunk * SUB, width),
                        green[b * subs + h, :, nc * take : (nc + 1) * take],
                        preferred_element_type=jnp.float32,
                    )
                    got = add if got is None else got + add
                at = pl.ds(pl.multiple_of(gh * depth + i * chunk * SUB, SUB), chunk * SUB)
                scores[at, :] += got
                return c

            lax.fori_loop(0, half_vectors // chunk, piece, 0)

            if slots < units:

                @pl.when(step + slots < units)
                def _():
                    start_load(step)

            return carry

        lax.fori_loop(0, units, contract, 0)

        own = (lax.broadcasted_iota(jnp.int32, (SUB, take), 1) & (SUB - 1)) == (
            lax.broadcasted_iota(jnp.int32, (SUB, take), 0)
        )
        lines = fb.shape[1]
        walker = lax.broadcasted_iota(jnp.int32, (walkers, lines, take), 0)
        line = lax.broadcasted_iota(jnp.int32, (walkers, lines, take), 1)
        source = (lax.broadcasted_iota(jnp.int32, (walkers, lines, take), 2) + nc * take) >> 3
        for q in range(groups_q):
            part = scores[q * span : (q + 1) * span, :].reshape(LANES, SUB, take)
            part = jnp.sum(jnp.where(own[None], part, 0.0), axis=1)
            pick = ((line == q) & (source == walker)) | (
                (line == groups_q + q) & (source == walkers + walker)
            )
            pick = pick.astype(jnp.float32).reshape(walkers * lines, take)
            fb[...] += lax.dot_general(
                pick, part, NT, preferred_element_type=jnp.float32, precision=lax.Precision.HIGHEST
            ).reshape(walkers, lines, LANES)

    peers(lambda p: send(fb.at[p], fb_all.at[me], 3, p))
    fb_all[me] = fb[me]
    wait_all(fb_all, recv_sem.at[3])
    summed = jnp.sum(fb_all[...], axis=0)
    for q in range(groups_q):
        for c in range(2):
            bias[c : c + 1, q * LANES : (q + 1) * LANES] = summed[
                c * groups_q + q : c * groups_q + q + 1
            ]

    wait_all(fall, send_sem.at[0])
    wait_all(gen_local, send_sem.at[1])
    wait_all(orb_rows, send_sem.at[2])
    wait_all(fb, send_sem.at[3])


def per_device(n, fields, chol, orbitals, trial):
    vectors, rows, width = chol.shape
    size, both = orbitals.shape[1:]
    row_block = min(16, rows)
    halves = 2
    units = (rows // row_block) * halves
    slots = min(4, units)
    q = vectors // LANES
    lines = -(-q // 8) * 8
    fb_lines = -(-2 * q // 8) * 8
    vmem = pl.BlockSpec(memory_space=pltpu.VMEM)
    bf16, f32 = jnp.bfloat16, jnp.float32
    out, bias = pl.pallas_call(
        functools.partial(kernel, n, halves, slots, row_block),
        out_shape=(
            jax.ShapeDtypeStruct((n, rows, both), bf16),
            jax.ShapeDtypeStruct((2, vectors), f32),
        ),
        in_specs=[vmem, pl.BlockSpec(memory_space=pl.ANY), vmem, vmem],
        out_specs=(vmem, vmem),
        scratch_shapes=[
            pltpu.VMEM((lines, LANES), f32),
            pltpu.VMEM((n, lines, LANES), f32),
            pltpu.VMEM((n * SUB, vectors * SUB), bf16),
            pltpu.VMEM((slots, vectors // halves, row_block, width), bf16),
            pltpu.VMEM((n, row_block, width), f32),
            pltpu.VMEM((n, rows, width), bf16),
            pltpu.VMEM((n, rows, width), bf16),
            pltpu.VMEM((size, both), f32),
            pltpu.VMEM((2, size, both), bf16),
            pltpu.VMEM((n, rows, both), bf16),
            pltpu.VMEM((n, row_block, both), f32),
            pltpu.VMEM((rows // SUB, width, 2 * n * SUB), bf16),
            pltpu.VMEM((vectors * SUB, min(2 * n * SUB, 256)), f32),
            pltpu.VMEM((n, fb_lines, LANES), f32),
            pltpu.VMEM((n, fb_lines, LANES), f32),
            pltpu.SemaphoreType.DMA((slots,)),
            pltpu.SemaphoreType.DMA((4,)),
            pltpu.SemaphoreType.DMA((4,)),
            pltpu.SemaphoreType.DMA((rows // row_block,)),
        ],
        compiler_params=pltpu.CompilerParams(
            collective_id=0, has_side_effects=True, vmem_limit_bytes=60 * 1024 * 1024
        ),
    )(fields, chol, orbitals[0], trial)
    return (
        out.reshape(1, size, both),
        bias.reshape(1, 2, vectors),
    )


def solution(mesh):
    in_specs = (
        P(("groups", "wide"), None),
        P(None, "wide", None),
        P(("groups", "wide"), None, None),
        P(),
    )
    out_specs = (P(("groups", "wide"), None, None), P(("groups", "wide"), None, None))
    return jax.shard_map(
        functools.partial(per_device, mesh.shape["wide"]),
        mesh=mesh, in_specs=in_specs, out_specs=out_specs, check_vma=False,
    )
```
